32 devices in a mesh: blk: 16 (over z, y, core), grp: 2 (over x).
Axes of the slice: x: 2, y: 2, z: 4, core: 2. Of those that a mesh axis runs over, the one named last changes fastest.
Arguments:
- entities: float32 [32768, 400], P('blk'), may hold values from -3 to 3
- relations: float32 [64, 400], replicated, may hold values from -1.8 to 1.8
- head_row: int32 [12288], P(('blk', 'grp')), may hold values from 0 to 2047
- relation_id: int32 [12288], P(('blk', 'grp')), may hold values from 0 to 63
- tail_owner: int32 [12288, 1], P(('blk', 'grp')), may hold values from 0 to 15; in each aligned block of 384 rows (0 to 383, 384 to 767, ...) at most 48 rows name the same one
- tail_row: int32 [12288], P(('blk', 'grp')), may hold values from 0 to 2047
- negative_rows: int32 [16, 64], P('blk'), may hold values from 0 to 2047
- edge_count: int32 [32], P(('blk', 'grp')), may hold values from 96 to 384, as said below
Outputs:
- new_entities: float32 [32768, 400], P('blk')
- new_relations: float32 [64, 400], replicated
The draws below stay inside these ranges and needn't reach their ends.
Inputs may be any that keep to these rules, and one draw needn't show every extreme that they name: `tail_owner`: among the 384 edge slots of one device no partition is named more than 48 times, a bound that some block reaches. `edge_count`: some device has all 384 slots live.
All inputs are finite; a program needn't handle non-finite values.
Results may differ from the reference program's by a relative error of at most 0.0003.
The reference program's roundings to bfloat16 on the way count: a program that leaves them out, or rounds other values in their place, can miss the bound.
Values may be sent and summed in bfloat16 or wider, within the bound.
A program may use at most 128 MiB of HBM per device.

```python
import math
import jax
import jax.numpy as jnp
import numpy as np
from jax import lax

D = 400
REL = 64
NEG = 64
EDGES = 384
ENT_DEV = 2048
CAP = 48
ENT = 32768
EDGES_ALL = 12288
N_BLK = 16
N_GRP = 2


def draw_edge_count(key, part):
    key = jax.random.fold_in(key, 7)
    first_key, second_key = jax.random.split(key)
    devices_all = N_BLK * N_GRP
    counts = jax.random.randint(first_key, (devices_all,), EDGES // 4, EDGES + 1)
    fullest = jax.random.randint(second_key, (), 0, devices_all)
    return jnp.where(jnp.arange(devices_all) == fullest, EDGES, counts).astype(jnp.int32)


def place_ends(entries, stream_key, least, high):
    longest = entries.shape.index(max(entries.shape))
    spots = []
    for shift in (0, 1):
        where = [jax.random.randint(jax.random.fold_in(stream_key, axis), (), 0, length) for axis, length in enumerate(entries.shape)]
        where[longest] = (where[longest] + shift) % entries.shape[longest]
        spots.append(tuple(where))
    return entries.at[spots[0]].set(least).at[spots[1]].set(high)


def shard_levels(own_key, shape, cuts, smallest, largest):
    gain = 1.0
    for axis_at, shards_of in cuts:
        steps = jax.random.uniform(jax.random.fold_in(jax.random.fold_in(own_key, 6), axis_at), (shards_of,), jnp.float32, smallest / len(cuts), largest / len(cuts))
        gain = gain * jnp.repeat(jnp.exp(steps), shape[axis_at] // shards_of).reshape((-1,) + (1,) * (len(shape) - 1 - axis_at))
    return gain


def routed_block(rng, own, number, rows, count, top, limit, skew):
    sequence = jax.random.permutation(rng, count)
    heavy_load, usual = shares(count, rows * top, limit, skew, True), shares(count, rows * top, limit, skew, False)
    places = jnp.arange(count)

    def named(sizes, offset_by):
        used = int((sizes > 0).sum())
        fixed = max(1, used // 4)
        passed = fixed + (places - fixed + offset_by * (used - fixed)) % max(1, count - fixed)
        return jnp.zeros((count,), jnp.int32).at[sequence[jnp.where(places < fixed, places, passed)]].set(jnp.asarray(sizes, jnp.int32))

    sizes = jnp.where(number % 4 == 0, named(heavy_load, number // 4), named(usual, number - number // 4 - 1))
    mixed = jax.random.permutation(jax.random.fold_in(own, 3), count)
    source_of, receiver = mixed[0:count // 2 * 2:2], mixed[1:count // 2 * 2:2]
    margin = jnp.minimum(sizes[source_of] - 1, limit - sizes[receiver]) // 2
    margin = jnp.where((source_of == sequence[0]) | (receiver == sequence[0]) | (sizes[receiver] == 0), 0, jnp.maximum(margin, 0))
    passed = jax.random.randint(jax.random.fold_in(own, 4), (count // 2,), 0, 1 << 20) % (margin + 1)
    sizes = sizes.at[source_of].add(-passed).at[receiver].add(passed)
    members = jnp.searchsorted(jnp.cumsum(sizes), jnp.arange(rows * top), side="right").astype(jnp.int32)
    listing = members.reshape(top, rows).T
    listing = listing[jax.random.permutation(jax.random.fold_in(own, 1), rows)]
    offset_by = jax.random.randint(jax.random.fold_in(own, 2), (rows, 1), 0, top)
    return jnp.take_along_axis(listing, (jnp.arange(top)[None, :] + offset_by) % top, axis=1)


def shares(number_of, total, reach, skew, full):
    weights = [(1 << 20) // math.isqrt(grade ** skew) + 1 for grade in range(1, number_of + 1)]
    largest = reach if full else min(reach, max(-(-total // number_of), total * weights[0] // sum(weights)))
    least = 1 if total - largest >= number_of - 1 else 0
    holding, surplus = [largest] + [least] * (number_of - 1), total - largest - least * (number_of - 1)
    while surplus > 0:
        movable = [i for i in range(1, number_of) if holding[i] < largest] or [i for i in range(1, number_of) if holding[i] < reach]
        whole, budget = sum([weights[i] for i in movable]), surplus
        for i in movable:
            addition = min(reach - holding[i], max(1, budget * weights[i] // whole), surplus)
            holding[i] = holding[i] + addition
            surplus = surplus - addition
    return np.array(holding)


def gaussian(stream_key, dims, deviation, most, pieces=(), held_as=jnp.bfloat16):
    factor_of = shard_levels(stream_key, dims, pieces, -0.22, 0.18) if pieces else 1.0
    values = jax.random.normal(stream_key, dims, jnp.float32) * deviation * factor_of
    return jnp.minimum(jnp.maximum(values, -most), most).astype(held_as)


def setup_inputs(seed: int = 0) -> dict:
    key_of = jax.random.split(jax.random.key(seed), 9)
    entities = gaussian(key_of[0], (ENT, D), 0.5, 3.0, ((0, 16),), jnp.float32)
    relations = gaussian(key_of[1], (REL, D), 0.3, 1.8, (), jnp.float32)
    head_row = place_ends(jax.random.randint(key_of[2], (EDGES_ALL,), 0, ENT_DEV), jax.random.fold_in(key_of[2], 1), 0, ENT_DEV - 1).astype(jnp.int32)
    relation_id = place_ends(jax.random.randint(key_of[3], (EDGES_ALL,), 0, REL), jax.random.fold_in(key_of[3], 1), 0, REL - 1).astype(jnp.int32)
    tail_owner_keys = jax.random.split(jax.random.fold_in(key_of[4], 1), EDGES_ALL // EDGES)
    tail_owner_turns = jax.random.permutation(jax.random.fold_in(key_of[4], 3), EDGES_ALL // EDGES)
    tail_owner = jax.vmap(lambda own, number: routed_block(jax.random.fold_in(key_of[4], 2), own, number, EDGES, N_BLK, 1, CAP, 2))(tail_owner_keys, tail_owner_turns).reshape((EDGES_ALL, 1))
    tail_row = place_ends(jax.random.randint(key_of[5], (EDGES_ALL,), 0, ENT_DEV), jax.random.fold_in(key_of[5], 1), 0, ENT_DEV - 1).astype(jnp.int32)
    negative_rows = place_ends(jax.random.randint(key_of[6], (N_BLK, NEG), 0, ENT_DEV), jax.random.fold_in(key_of[6], 1), 0, ENT_DEV - 1).astype(jnp.int32)
    edge_count = draw_edge_count(jax.random.fold_in(key_of[8], 71), 0)
    return {"entities": entities, "relations": relations, "head_row": head_row, "relation_id": relation_id, "tail_owner": tail_owner, "tail_row": tail_row, "negative_rows": negative_rows, "edge_count": edge_count}


EPSILON = 1e-06
LEARN_RATE = 0.3

def rounded(values):
    return lax.optimization_barrier(values.astype(jnp.bfloat16)).astype(jnp.float32)

def complex_product(factor, other):
    half_width = factor.shape[1] // 2
    factor_real, factor_imag = (factor[:, :half_width], factor[:, half_width:])
    other_real, other_imag = (other[:, :half_width], other[:, half_width:])
    return jnp.concatenate([factor_real * other_real - factor_imag * other_imag, factor_real * other_imag + factor_imag * other_real], axis=1)

def complex_grads(upstream, head_vals, rel_vals):
    half_width = upstream.shape[1] // 2
    grad_real, grad_imag = (upstream[:, :half_width], upstream[:, half_width:])
    head_real, head_imag = (head_vals[:, :half_width], head_vals[:, half_width:])
    rel_real, rel_imag = (rel_vals[:, :half_width], rel_vals[:, half_width:])
    grad_head = jnp.concatenate([grad_real * rel_real + grad_imag * rel_imag, grad_imag * rel_real - grad_real * rel_imag], axis=1)
    grad_rel = jnp.concatenate([grad_real * head_real + grad_imag * head_imag, grad_imag * head_real - grad_real * head_imag], axis=1)
    return (grad_head, grad_rel)

def adagrad(table, table_grads):
    square_mean = lax.optimization_barrier(jnp.mean(table_grads * table_grads, axis=1, keepdims=True))
    return table - LEARN_RATE * table_grads / (jnp.sqrt(square_mean) + EPSILON)

def reference(entities, relations, head_row, relation_id, tail_owner, tail_row, negative_rows, edge_count):
    edge_index = jnp.arange(EDGES_ALL, dtype=jnp.int32)
    device = (edge_index // EDGES).astype(jnp.int32)
    partition = (device // N_GRP).astype(jnp.int32)
    head_glob = (partition * ENT_DEV + head_row).astype(jnp.int32)
    tail_glob = (tail_owner[:, 0] * ENT_DEV + tail_row).astype(jnp.int32)
    live = (edge_index % EDGES < edge_count[device]).astype(jnp.float32)
    head_vals = rounded(entities[head_glob])
    tail_vals = rounded(entities[tail_glob])
    rel_rows = relations[relation_id]
    query_vals = rounded(complex_product(head_vals, rel_rows))
    positive = lax.optimization_barrier(jnp.sum(query_vals * tail_vals, axis=1))
    weight = -live * jax.nn.sigmoid(-positive)
    grad_tail = weight[:, None] * query_vals
    neg_glob = (jnp.arange(N_BLK, dtype=jnp.int32)[:, None] * ENT_DEV + negative_rows).astype(jnp.int32)
    neg_blocks = entities[neg_glob]
    neg_scale = 1.0 / (N_BLK * NEG)

    def score_block(grad_query, neg_block):
        block_vals = rounded(neg_block)
        scores = jnp.dot(query_vals, block_vals.T, precision=lax.Precision.HIGHEST)
        nweight = rounded(neg_scale * live[:, None] * jax.nn.sigmoid(scores))
        grad_query = grad_query + jnp.dot(nweight, block_vals, precision=lax.Precision.HIGHEST)
        block_grad = jnp.dot(nweight.T, query_vals, precision=lax.Precision.HIGHEST)
        return (grad_query, block_grad)
    grad_query, neg_grads = lax.scan(score_block, weight[:, None] * tail_vals, neg_blocks)
    grad_head, grad_rel = complex_grads(grad_query, head_vals, rel_rows)
    entity_grads = jnp.zeros((ENT, D), jnp.float32)
    entity_grads = entity_grads.at[head_glob].add(grad_head)
    entity_grads = entity_grads.at[tail_glob].add(grad_tail)
    entity_grads = entity_grads.at[neg_glob.reshape(-1)].add(neg_grads.reshape(-1, D))
    relation_grads = jnp.zeros((REL, D), jnp.float32).at[relation_id].add(grad_rel)
    return (adagrad(entities, entity_grads), adagrad(relations, relation_grads))
```

```python
import jax
import jax.numpy as jnp
from jax import lax
from jax.sharding import PartitionSpec as P

EPSILON = 1e-06
LEARN_RATE = 0.3
NEG_TYPE = jnp.bfloat16


def complex_product(factor, other):
    half_width = factor.shape[1] // 2
    factor_real, factor_imag = (factor[:, :half_width], factor[:, half_width:])
    other_real, other_imag = (other[:, :half_width], other[:, half_width:])
    return jnp.concatenate(
        [
            factor_real * other_real - factor_imag * other_imag,
            factor_real * other_imag + factor_imag * other_real,
        ],
        axis=1,
    )


def complex_grads(upstream, head_vals, rel_vals):
    half_width = upstream.shape[1] // 2
    grad_real, grad_imag = (upstream[:, :half_width], upstream[:, half_width:])
    head_real, head_imag = (head_vals[:, :half_width], head_vals[:, half_width:])
    rel_real, rel_imag = (rel_vals[:, :half_width], rel_vals[:, half_width:])
    grad_head = jnp.concatenate(
        [grad_real * rel_real + grad_imag * rel_imag, grad_imag * rel_real - grad_real * rel_imag],
        axis=1,
    )
    grad_rel = jnp.concatenate(
        [
            grad_real * head_real + grad_imag * head_imag,
            grad_imag * head_real - grad_real * head_imag,
        ],
        axis=1,
    )
    return (grad_head, grad_rel)


def adagrad(table, table_grads):
    square_mean = jnp.mean(table_grads * table_grads, axis=1, keepdims=True)
    return table - LEARN_RATE * table_grads / (jnp.sqrt(square_mean) + EPSILON)


def hot_rows(index, count, dtype):
    return (index[:, None] == jnp.arange(count, dtype=jnp.int32)[None, :]).astype(dtype)


def pick(hot, table):
    return jnp.dot(hot, table, preferred_element_type=jnp.float32).astype(jnp.bfloat16)


def spread(rows, count, grads):
    hot = hot_rows(rows, count, jnp.bfloat16)
    high = lax.reduce_precision(grads, 8, 7)
    both = jnp.concatenate([high, grads - high], axis=1).astype(jnp.bfloat16)
    sums = lax.dot_general(
        hot, both, (((0,), (0,)), ((), ())), preferred_element_type=jnp.float32
    )
    width = grads.shape[1]
    return sums[:, :width] + sums[:, width:]


def swap(own):
    pairs = [(i, (i + 1) % lax.axis_size("grp")) for i in range(lax.axis_size("grp"))]
    other = lax.ppermute(own, "grp", pairs)
    first = lax.axis_index("grp") == 0
    return jnp.concatenate([jnp.where(first, own, other), jnp.where(first, other, own)], axis=0)


def deal(blocks, axes):
    return lax.all_to_all(blocks, axes, split_axis=0, concat_axis=0, tiled=True)


def per_device(
    entities, relations, head_row, relation_id, tail_owner, tail_row, negative_rows, edge_count
):
    owners = lax.axis_size("blk")
    devices = owners * lax.axis_size("grp")
    edge_total = head_row.shape[0]
    ent_count, row_width = entities.shape
    neg_count = negative_rows.shape[1]
    rel_count = relations.shape[0]
    capacity = max(2, 2 * edge_total // owners)
    alive = jnp.arange(edge_total, dtype=jnp.int32) < edge_count[0]
    live = alive.astype(jnp.float32)
    target = tail_owner[:, 0]
    target_hot = hot_rows(target, owners, jnp.float32)
    order = jnp.arange(edge_total, dtype=jnp.int32)
    before = (order[:, None] > order[None, :]).astype(jnp.bfloat16)
    earlier = jnp.dot(before, target_hot.astype(jnp.bfloat16), preferred_element_type=jnp.float32)
    slot_index = jnp.sum(earlier * target_hot, axis=1).astype(jnp.int32)
    position = target * capacity + slot_index
    slot_hot = hot_rows(position, owners * capacity, jnp.bfloat16)
    wanted = jnp.where(alive, tail_row, -1)
    taken = hot_rows(position, owners * capacity, jnp.int32)
    requests = jnp.sum(taken * (wanted + 1)[:, None], axis=0) - 1
    requested = deal(requests.reshape(owners, capacity), "blk").reshape(-1)

    table = entities.astype(jnp.bfloat16)
    own_block = pick(hot_rows(negative_rows[0], ent_count, jnp.bfloat16), table)
    piece = lax.all_gather(own_block, "blk", axis=0, tiled=True)
    located = pick(hot_rows(requested, ent_count, jnp.bfloat16), table)
    arrived = deal(located.reshape(owners, capacity, row_width), "blk")

    head_bf = pick(hot_rows(head_row, ent_count, jnp.bfloat16), table)
    rel_onehot = hot_rows(relation_id, rel_count, jnp.float32)
    rel_rows = jnp.dot(rel_onehot, relations, precision=lax.Precision.HIGHEST)
    head_f = head_bf.astype(jnp.float32)
    query_bf = complex_product(head_f, rel_rows).astype(jnp.bfloat16)
    query_f = query_bf.astype(jnp.float32)
    outgoing = lax.dot_general(
        slot_hot, query_bf, (((0,), (0,)), ((), ())), preferred_element_type=jnp.float32
    ).astype(jnp.bfloat16)
    returned = deal(outgoing.reshape(owners, capacity, row_width), "blk").reshape(-1, row_width)

    neg_scale = 1.0 / (owners * neg_count)
    scores = jnp.dot(query_bf, piece.T, preferred_element_type=jnp.float32)
    nweight = (neg_scale * live[:, None] * jax.nn.sigmoid(scores)).astype(jnp.bfloat16)
    neg_query = jnp.dot(nweight, piece, preferred_element_type=jnp.float32)
    neg_grads = jnp.dot(nweight.T, query_bf, preferred_element_type=jnp.float32)
    neg_parts = deal(neg_grads.astype(NEG_TYPE).reshape(owners, neg_count, row_width), "blk")
    neg_sum = jnp.sum(neg_parts.astype(jnp.float32), axis=0)

    tail_bf = pick(slot_hot, arrived.reshape(owners * capacity, row_width))
    tail_f = tail_bf.astype(jnp.float32)
    weight = -live * jax.nn.sigmoid(-jnp.sum(query_f * tail_f, axis=1))
    grad_query = weight[:, None] * tail_f + neg_query
    grad_head, grad_rel = complex_grads(grad_query, head_f, rel_rows)
    rel_local = jnp.dot(rel_onehot.T, grad_rel, precision=lax.Precision.HIGHEST)
    rel_parts = deal(rel_local.reshape(devices, -1), ("blk", "grp"))
    rel_share = jnp.sum(rel_parts, axis=0)
    rel_total = deal(jnp.broadcast_to(rel_share[None], rel_parts.shape), ("blk", "grp"))
    new_relations = adagrad(relations, rel_total.reshape(rel_count, row_width))

    returned_f = returned.astype(jnp.float32)
    owner_weight = -jax.nn.sigmoid(-jnp.sum(returned_f * located.astype(jnp.float32), axis=1))
    tail_rows = swap(requested)
    tail_weights = swap(owner_weight)
    tail_grads = tail_weights[:, None] * swap(returned).astype(jnp.float32)
    entity_grads = spread(tail_rows, ent_count, tail_grads)
    late_rows = jnp.concatenate([head_row, negative_rows[0]])
    late = swap(jnp.concatenate([grad_head, neg_sum], axis=0))
    entity_grads = entity_grads + spread(swap(late_rows), ent_count, late)
    new_entities = adagrad(entities, entity_grads)
    return (new_entities, new_relations)


def solution(mesh):
    return jax.shard_map(
        per_device,
        mesh=mesh,
        in_specs=(
            P("blk", None),
            P(),
            P(("blk", "grp")),
            P(("blk", "grp")),
            P(("blk", "grp"), None),
            P(("blk", "grp")),
            P("blk", None),
            P(("blk", "grp")),
        ),
        out_specs=(P("blk", None), P()),
        check_vma=False,
    )
```

```python
import functools
import jax
import jax.numpy as jnp
from jax import lax
from jax.experimental import pallas as pl
from jax.experimental.pallas import tpu as pltpu
from jax.sharding import PartitionSpec as P

EPSILON = 1e-06
LEARN_RATE = 0.3
NEG_TYPE = jnp.bfloat16


def complex_product(factor, other):
    half_width = factor.shape[1] // 2
    factor_real, factor_imag = (factor[:, :half_width], factor[:, half_width:])
    other_real, other_imag = (other[:, :half_width], other[:, half_width:])
    return jnp.concatenate(
        [
            factor_real * other_real - factor_imag * other_imag,
            factor_real * other_imag + factor_imag * other_real,
        ],
        axis=1,
    )


def complex_grads(upstream, head_vals, rel_vals):
    half_width = upstream.shape[1] // 2
    grad_real, grad_imag = (upstream[:, :half_width], upstream[:, half_width:])
    head_real, head_imag = (head_vals[:, :half_width], head_vals[:, half_width:])
    rel_real, rel_imag = (rel_vals[:, :half_width], rel_vals[:, half_width:])
    grad_head = jnp.concatenate(
        [grad_real * rel_real + grad_imag * rel_imag, grad_imag * rel_real - grad_real * rel_imag],
        axis=1,
    )
    grad_rel = jnp.concatenate(
        [
            grad_real * head_real + grad_imag * head_imag,
            grad_imag * head_real - grad_real * head_imag,
        ],
        axis=1,
    )
    return (grad_head, grad_rel)


def adagrad(table, table_grads):
    square_mean = jnp.mean(table_grads * table_grads, axis=1, keepdims=True)
    return table - LEARN_RATE * table_grads / (jnp.sqrt(square_mean) + EPSILON)


def hot_rows(index, count, dtype):
    return (index[:, None] == jnp.arange(count, dtype=jnp.int32)[None, :]).astype(dtype)


def pick(hot, table):
    return jnp.dot(hot, table, preferred_element_type=jnp.float32).astype(jnp.bfloat16)


def spread(rows, count, grads):
    hot = hot_rows(rows, count, jnp.bfloat16)
    high = lax.reduce_precision(grads, 8, 7)
    both = jnp.concatenate([high, grads - high], axis=1).astype(jnp.bfloat16)
    sums = lax.dot_general(
        hot, both, (((0,), (0,)), ((), ())), preferred_element_type=jnp.float32
    )
    width = grads.shape[1]
    return sums[:, :width] + sums[:, width:]


def swap(own):
    pairs = [(i, (i + 1) % lax.axis_size("grp")) for i in range(lax.axis_size("grp"))]
    other = lax.ppermute(own, "grp", pairs)
    first = lax.axis_index("grp") == 0
    return jnp.concatenate([jnp.where(first, own, other), jnp.where(first, other, own)], axis=0)


def deal(blocks, axes):
    return lax.all_to_all(blocks, axes, split_axis=0, concat_axis=0, tiled=True)


def remote(source, landing, send_sem, recv_sem, device):
    return pltpu.make_async_remote_copy(
        src_ref=source,
        dst_ref=landing,
        send_sem=send_sem,
        recv_sem=recv_sem,
        device_id=device,
        device_id_type=pl.DeviceIdType.MESH,
    )


def forward_kernel(
    owners, query_ref, tail_ref, own_ref, query_out, tail_out, neg_out, sends, recvs, passes, gots
):
    me = lax.axis_index("blk")
    sibling = me + 1 - 2 * lax.rem(me, 2)
    chips = owners // 2
    barrier = pltpu.get_barrier_semaphore()

    def hello(step, carry):
        pl.semaphore_signal(
            barrier,
            inc=1,
            device_id={"blk": lax.rem(me + step, owners)},
            device_id_type=pl.DeviceIdType.MESH,
        )
        return carry

    lax.fori_loop(1, owners, hello, 0)
    pl.semaphore_wait(barrier, owners - 1)

    def neg_copy(step):
        return remote(
            own_ref,
            neg_out.at[me],
            sends.at[0, step],
            recvs.at[0, step],
            {"blk": lax.rem(me + 2 * step, owners)},
        )

    def pass_copy(step):
        block = lax.rem(me - 2 * step + 2 * owners, owners)
        source = neg_out.at[block]
        return remote(source, source, passes.at[step], gots.at[step], {"blk": sibling})

    def row_copy(kind, source, landing, step):
        there = lax.rem(me + step, owners)
        return remote(
            source.at[there],
            landing.at[me],
            sends.at[kind, step],
            recvs.at[kind, step],
            {"blk": there},
        )

    def each(low, high, act):
        def body(step, carry):
            act(step)
            return carry

        lax.fori_loop(low, high, body, 0)

    neg_out[me] = own_ref[...]
    each(1, chips, lambda step: neg_copy(step).start())
    pass_copy(0).start()
    each(1, owners, lambda step: row_copy(1, tail_ref, tail_out, step).start())
    each(1, owners, lambda step: row_copy(2, query_ref, query_out, step).start())
    tail_out[me] = tail_ref[me]
    query_out[me] = query_ref[me]

    def hand_on(step):
        neg_copy(step).wait_recv()
        pass_copy(step).start()

    each(1, chips, hand_on)

    def finish(step):
        row_copy(1, tail_ref, tail_out, step).wait()
        row_copy(2, query_ref, query_out, step).wait()

    each(0, chips, lambda step: pass_copy(step).wait())
    each(1, chips, lambda step: neg_copy(step).wait_send())
    each(1, owners, finish)


def forward_exchange(outgoing, located, own_block):
    owners = outgoing.shape[0]
    vmem = pl.BlockSpec(memory_space=pltpu.VMEM)
    return pl.pallas_call(
        functools.partial(forward_kernel, owners),
        out_shape=(
            jax.ShapeDtypeStruct(outgoing.shape, jnp.bfloat16),
            jax.ShapeDtypeStruct(located.shape, jnp.bfloat16),
            jax.ShapeDtypeStruct((owners,) + own_block.shape, jnp.bfloat16),
        ),
        in_specs=[vmem] * 3,
        out_specs=(vmem,) * 3,
        scratch_shapes=[
            pltpu.SemaphoreType.DMA((3, owners)),
            pltpu.SemaphoreType.DMA((3, owners)),
            pltpu.SemaphoreType.DMA((owners,)),
            pltpu.SemaphoreType.DMA((owners,)),
        ],
        compiler_params=pltpu.CompilerParams(
            collective_id=1, has_side_effects=True, vmem_limit_bytes=48 * 2**20
        ),
    )(outgoing, located, own_block)


def per_device(
    entities, relations, head_row, relation_id, tail_owner, tail_row, negative_rows, edge_count
):
    owners = lax.axis_size("blk")
    devices = owners * lax.axis_size("grp")
    edge_total = head_row.shape[0]
    ent_count, row_width = entities.shape
    neg_count = negative_rows.shape[1]
    rel_count = relations.shape[0]
    capacity = -(-max(2, 2 * edge_total // owners) // 16) * 16
    alive = jnp.arange(edge_total, dtype=jnp.int32) < edge_count[0]
    live = alive.astype(jnp.float32)
    target = tail_owner[:, 0]
    target_hot = hot_rows(target, owners, jnp.float32)
    order = jnp.arange(edge_total, dtype=jnp.int32)
    before = (order[:, None] > order[None, :]).astype(jnp.bfloat16)
    earlier = jnp.dot(before, target_hot.astype(jnp.bfloat16), preferred_element_type=jnp.float32)
    slot_index = jnp.sum(earlier * target_hot, axis=1).astype(jnp.int32)
    position = target * capacity + slot_index
    slot_hot = hot_rows(position, owners * capacity, jnp.bfloat16)
    wanted = jnp.where(alive, tail_row, -1)
    taken = hot_rows(position, owners * capacity, jnp.int32)
    requests = jnp.sum(taken * (wanted + 1)[:, None], axis=0) - 1
    requested = deal(requests.reshape(owners, capacity), "blk").reshape(-1)

    table = entities.astype(jnp.bfloat16)
    own_block = pick(hot_rows(negative_rows[0], ent_count, jnp.bfloat16), table)
    located = pick(hot_rows(requested, ent_count, jnp.bfloat16), table)

    head_bf = pick(hot_rows(head_row, ent_count, jnp.bfloat16), table)
    rel_onehot = hot_rows(relation_id, rel_count, jnp.float32)
    rel_rows = jnp.dot(rel_onehot, relations, precision=lax.Precision.HIGHEST)
    head_f = head_bf.astype(jnp.float32)
    query_bf = complex_product(head_f, rel_rows).astype(jnp.bfloat16)
    query_f = query_bf.astype(jnp.float32)
    outgoing = lax.dot_general(
        slot_hot, query_bf, (((0,), (0,)), ((), ())), preferred_element_type=jnp.float32
    ).astype(jnp.bfloat16)
    returned, arrived, piece = forward_exchange(
        outgoing.reshape(owners, capacity, row_width),
        located.reshape(owners, capacity, row_width),
        own_block,
    )
    returned = returned.reshape(-1, row_width)
    piece = piece.reshape(-1, row_width)

    neg_scale = 1.0 / (owners * neg_count)
    scores = jnp.dot(query_bf, piece.T, preferred_element_type=jnp.float32)
    nweight = (neg_scale * live[:, None] * jax.nn.sigmoid(scores)).astype(jnp.bfloat16)
    neg_query = jnp.dot(nweight, piece, preferred_element_type=jnp.float32)
    neg_grads = jnp.dot(nweight.T, query_bf, preferred_element_type=jnp.float32)
    neg_parts = deal(neg_grads.astype(NEG_TYPE).reshape(owners, neg_count, row_width), "blk")
    neg_sum = jnp.sum(neg_parts.astype(jnp.float32), axis=0)

    tail_bf = pick(slot_hot, arrived.reshape(owners * capacity, row_width))
    tail_f = tail_bf.astype(jnp.float32)
    weight = -live * jax.nn.sigmoid(-jnp.sum(query_f * tail_f, axis=1))
    grad_query = weight[:, None] * tail_f + neg_query
    grad_head, grad_rel = complex_grads(grad_query, head_f, rel_rows)
    rel_local = jnp.dot(rel_onehot.T, grad_rel, precision=lax.Precision.HIGHEST)
    rel_parts = deal(rel_local.reshape(devices, -1), ("blk", "grp"))
    rel_share = jnp.sum(rel_parts, axis=0)
    rel_total = deal(jnp.broadcast_to(rel_share[None], rel_parts.shape), ("blk", "grp"))
    new_relations = adagrad(relations, rel_total.reshape(rel_count, row_width))

    returned_f = returned.astype(jnp.float32)
    owner_weight = -jax.nn.sigmoid(-jnp.sum(returned_f * located.astype(jnp.float32), axis=1))
    tail_rows = swap(requested)
    tail_weights = swap(owner_weight)
    tail_grads = tail_weights[:, None] * swap(returned).astype(jnp.float32)
    entity_grads = spread(tail_rows, ent_count, tail_grads)
    late_rows = jnp.concatenate([head_row, negative_rows[0]])
    late = swap(jnp.concatenate([grad_head, neg_sum], axis=0))
    entity_grads = entity_grads + spread(swap(late_rows), ent_count, late)
    new_entities = adagrad(entities, entity_grads)
    return (new_entities, new_relations)


def solution(mesh):
    return jax.shard_map(
        per_device,
        mesh=mesh,
        in_specs=(
            P("blk", None),
            P(),
            P(("blk", "grp")),
            P(("blk", "grp")),
            P(("blk", "grp"), None),
            P(("blk", "grp")),
            P("blk", None),
            P(("blk", "grp")),
        ),
        out_specs=(P("blk", None), P()),
        check_vma=False,
    )
```

```python
import functools
import jax
import jax.numpy as jnp
from jax import lax
from jax.experimental import pallas as pl
from jax.experimental.pallas import tpu as pltpu
from jax.sharding import PartitionSpec as P

EPSILON = 1e-06
LEARN_RATE = 0.3


def complex_product(factor, other):
    half_width = factor.shape[1] // 2
    factor_real, factor_imag = (factor[:, :half_width], factor[:, half_width:])
    other_real, other_imag = (other[:, :half_width], other[:, half_width:])
    return jnp.concatenate(
        [
            factor_real * other_real - factor_imag * other_imag,
            factor_real * other_imag + factor_imag * other_real,
        ],
        axis=1,
    )


def complex_grads(upstream, head_vals, rel_vals):
    half_width = upstream.shape[1] // 2
    grad_real, grad_imag = (upstream[:, :half_width], upstream[:, half_width:])
    head_real, head_imag = (head_vals[:, :half_width], head_vals[:, half_width:])
    rel_real, rel_imag = (rel_vals[:, :half_width], rel_vals[:, half_width:])
    grad_head = jnp.concatenate(
        [grad_real * rel_real + grad_imag * rel_imag, grad_imag * rel_real - grad_real * rel_imag],
        axis=1,
    )
    grad_rel = jnp.concatenate(
        [
            grad_real * head_real + grad_imag * head_imag,
            grad_imag * head_real - grad_real * head_imag,
        ],
        axis=1,
    )
    return (grad_head, grad_rel)


def adagrad(table, table_grads):
    square_mean = jnp.mean(table_grads * table_grads, axis=1, keepdims=True)
    return table - LEARN_RATE * table_grads / (jnp.sqrt(square_mean) + EPSILON)


def hot_rows(index, count, dtype):
    return (index[:, None] == jnp.arange(count, dtype=jnp.int32)[None, :]).astype(dtype)


def pick(hot, table):
    return jnp.dot(hot, table, preferred_element_type=jnp.float32).astype(jnp.bfloat16)


def spread(rows, count, grads):
    hot = hot_rows(rows, count, jnp.bfloat16)
    high = lax.reduce_precision(grads, 8, 7)
    both = jnp.concatenate([high, grads - high], axis=1).astype(jnp.bfloat16)
    sums = lax.dot_general(
        hot, both, (((0,), (0,)), ((), ())), preferred_element_type=jnp.float32
    )
    width = grads.shape[1]
    return sums[:, :width] + sums[:, width:]


def swap(own):
    pairs = [(i, (i + 1) % lax.axis_size("grp")) for i in range(lax.axis_size("grp"))]
    other = lax.ppermute(own, "grp", pairs)
    first = lax.axis_index("grp") == 0
    return jnp.concatenate([jnp.where(first, own, other), jnp.where(first, other, own)], axis=0)


def deal(blocks, axes):
    return lax.all_to_all(blocks, axes, split_axis=0, concat_axis=0, tiled=True)


def remote(source, landing, send_sem, recv_sem, device):
    return pltpu.make_async_remote_copy(
        src_ref=source,
        dst_ref=landing,
        send_sem=send_sem,
        recv_sem=recv_sem,
        device_id=device,
        device_id_type=pl.DeviceIdType.MESH,
    )


def forward_kernel(
    owners, query_ref, tail_ref, own_ref, query_out, tail_out, neg_out, sends, recvs, passes, gots
):
    me = lax.axis_index("blk")
    sibling = me + 1 - 2 * lax.rem(me, 2)
    chips = owners // 2
    barrier = pltpu.get_barrier_semaphore()

    def hello(step, carry):
        pl.semaphore_signal(
            barrier,
            inc=1,
            device_id={"blk": lax.rem(me + step, owners)},
            device_id_type=pl.DeviceIdType.MESH,
        )
        return carry

    lax.fori_loop(1, owners, hello, 0)
    pl.semaphore_wait(barrier, owners - 1)

    def neg_copy(step):
        return remote(
            own_ref,
            neg_out.at[me],
            sends.at[0, step],
            recvs.at[0, step],
            {"blk": lax.rem(me + 2 * step, owners)},
        )

    def pass_copy(step):
        block = lax.rem(me - 2 * step + 2 * owners, owners)
        source = neg_out.at[block]
        return remote(source, source, passes.at[step], gots.at[step], {"blk": sibling})

    def row_copy(kind, source, landing, step):
        there = lax.rem(me + step, owners)
        return remote(
            source.at[there],
            landing.at[me],
            sends.at[kind, step],
            recvs.at[kind, step],
            {"blk": there},
        )

    def each(low, high, act):
        def body(step, carry):
            act(step)
            return carry

        lax.fori_loop(low, high, body, 0)

    neg_out[me] = own_ref[...]
    each(1, chips, lambda step: neg_copy(step).start())
    pass_copy(0).start()
    each(1, owners, lambda step: row_copy(1, tail_ref, tail_out, step).start())
    each(1, owners, lambda step: row_copy(2, query_ref, query_out, step).start())
    tail_out[me] = tail_ref[me]
    query_out[me] = query_ref[me]

    def hand_on(step):
        neg_copy(step).wait_recv()
        pass_copy(step).start()

    each(1, chips, hand_on)

    def finish(step):
        row_copy(1, tail_ref, tail_out, step).wait()
        row_copy(2, query_ref, query_out, step).wait()

    each(0, chips, lambda step: pass_copy(step).wait())
    each(1, chips, lambda step: neg_copy(step).wait_send())
    each(1, owners, finish)


def forward_exchange(outgoing, located, own_block):
    owners = outgoing.shape[0]
    vmem = pl.BlockSpec(memory_space=pltpu.VMEM)
    return pl.pallas_call(
        functools.partial(forward_kernel, owners),
        out_shape=(
            jax.ShapeDtypeStruct(outgoing.shape, jnp.bfloat16),
            jax.ShapeDtypeStruct(located.shape, jnp.bfloat16),
            jax.ShapeDtypeStruct((owners,) + own_block.shape, jnp.bfloat16),
        ),
        in_specs=[vmem] * 3,
        out_specs=(vmem,) * 3,
        scratch_shapes=[
            pltpu.SemaphoreType.DMA((3, owners)),
            pltpu.SemaphoreType.DMA((3, owners)),
            pltpu.SemaphoreType.DMA((owners,)),
            pltpu.SemaphoreType.DMA((owners,)),
        ],
        compiler_params=pltpu.CompilerParams(
            collective_id=1, has_side_effects=True, vmem_limit_bytes=48 * 2**20
        ),
    )(outgoing, located, own_block)


def backward_kernel(
    owners,
    bits,
    neg_ref,
    rel_ref,
    head_ref,
    late_out,
    rel_out,
    pre,
    staged,
    landed,
    rel_sums,
    rel_got,
    pre_send,
    pre_recv,
    part_send,
    part_recv,
    rel_send,
    rel_recv,
    grp_send,
    grp_recv,
):
    me = lax.axis_index("blk")
    group = lax.axis_index("grp")
    mate = {"grp": 1 - group}
    core = lax.rem(me, 2)
    chip = me // 2
    sibling = me + 1 - 2 * core
    chips = owners // 2
    head_count = head_ref.shape[0]
    neg_count = neg_ref.shape[1]
    barrier = pltpu.get_barrier_semaphore()

    def each(low, high, act):
        def body(step, carry):
            act(step)
            return carry

        lax.fori_loop(low, high, body, 0)

    def hello(step):
        pl.semaphore_signal(
            barrier,
            inc=1,
            device_id={"blk": lax.rem(me + step, owners)},
            device_id_type=pl.DeviceIdType.MESH,
        )

    each(1, owners, hello)
    pl.semaphore_signal(barrier, inc=1, device_id=mate, device_id_type=pl.DeviceIdType.MESH)
    pl.semaphore_wait(barrier, owners)

    def rel_copy(turn):
        if turn == 0:
            device = mate
        else:
            bit = 2 ** (turn - 1)
            device = {"blk": me + bit - 2 * bit * lax.rem(me // bit, 2)}
        source = rel_ref if turn == 0 else rel_sums.at[turn - 1]
        return remote(source, rel_got.at[turn], rel_send.at[turn], rel_recv.at[turn], device)

    def rel_turn(turn):
        rel_copy(turn).wait_recv()
        source = rel_ref[...] if turn == 0 else rel_sums[turn - 1]
        if turn < bits:
            rel_sums[turn] = source + rel_got[turn]
            rel_copy(turn + 1).start()
        else:
            rel_out[...] = source + rel_got[turn]

    def pre_copy(step):
        there = lax.rem(chip + step, chips)
        return remote(
            neg_ref.at[2 * there + 1 - core],
            pre.at[there],
            pre_send.at[step],
            pre_recv.at[step],
            {"blk": sibling},
        )

    def part_copy(step):
        there = lax.rem(chip + step, chips)
        return remote(
            staged.at[there],
            landed.at[chip],
            part_send.at[step],
            part_recv.at[step],
            {"blk": 2 * there + core},
        )

    head_rows = late_out.at[group, pl.ds(0, head_count)]
    head_copy = remote(head_ref, head_rows, grp_send.at[0], grp_recv.at[0], mate)
    sum_rows = late_out.at[group, pl.ds(head_count, neg_count)]
    sum_copy = remote(sum_rows, sum_rows, grp_send.at[1], grp_recv.at[1], mate)

    rel_copy(0).start()
    each(0, chips, lambda step: pre_copy(step).start())
    head_copy.start()
    late_out[group, pl.ds(0, head_count)] = head_ref[...]
    rel_turn(0)

    def part(step):
        there = lax.rem(chip + step, chips)
        pre_copy(step).wait_recv()
        staged[there] = (neg_ref[2 * there + core] + pre[there]).astype(jnp.bfloat16)
        part_copy(step).start()

    each(1, chips, part)
    for turn in range(1, bits + 1):
        rel_turn(turn)
    pre_copy(0).wait_recv()
    late_out[group, pl.ds(head_count, neg_count)] = neg_ref[me] + pre[chip]

    def add(step):
        part_copy(step).wait_recv()
        origin = lax.rem(chip - step + chips, chips)
        late_out[group, pl.ds(head_count, neg_count)] += landed[origin].astype(jnp.float32)

    each(1, chips, add)
    sum_copy.start()
    for turn in range(bits + 1):
        rel_copy(turn).wait_send()
    each(0, chips, lambda step: pre_copy(step).wait_send())
    each(1, chips, lambda step: part_copy(step).wait_send())
    head_copy.wait()
    sum_copy.wait()


def backward_exchange(neg_parts, rel_local, grad_head):
    owners, neg_count, width = neg_parts.shape
    bits = owners.bit_length() - 1
    chips = owners // 2
    vmem = pl.BlockSpec(memory_space=pltpu.VMEM)
    late_count = grad_head.shape[0] + neg_count
    return pl.pallas_call(
        functools.partial(backward_kernel, owners, bits),
        out_shape=(
            jax.ShapeDtypeStruct((2, late_count, width), jnp.float32),
            jax.ShapeDtypeStruct(rel_local.shape, jnp.float32),
        ),
        in_specs=[vmem] * 3,
        out_specs=(vmem,) * 2,
        scratch_shapes=[
            pltpu.VMEM((chips, neg_count, width), jnp.float32),
            pltpu.VMEM((chips, neg_count, width), jnp.bfloat16),
            pltpu.VMEM((chips, neg_count, width), jnp.bfloat16),
            pltpu.VMEM((bits + 1,) + rel_local.shape, jnp.float32),
            pltpu.VMEM((bits + 1,) + rel_local.shape, jnp.float32),
            pltpu.SemaphoreType.DMA((chips,)),
            pltpu.SemaphoreType.DMA((chips,)),
            pltpu.SemaphoreType.DMA((chips,)),
            pltpu.SemaphoreType.DMA((chips,)),
            pltpu.SemaphoreType.DMA((bits + 1,)),
            pltpu.SemaphoreType.DMA((bits + 1,)),
            pltpu.SemaphoreType.DMA((2,)),
            pltpu.SemaphoreType.DMA((2,)),
        ],
        compiler_params=pltpu.CompilerParams(
            collective_id=2, has_side_effects=True, vmem_limit_bytes=48 * 2**20
        ),
    )(neg_parts, rel_local, grad_head)


def per_device(
    entities, relations, head_row, relation_id, tail_owner, tail_row, negative_rows, edge_count
):
    owners = lax.axis_size("blk")
    edge_total = head_row.shape[0]
    ent_count, row_width = entities.shape
    neg_count = negative_rows.shape[1]
    rel_count = relations.shape[0]
    capacity = -(-max(2, 2 * edge_total // owners) // 16) * 16
    alive = jnp.arange(edge_total, dtype=jnp.int32) < edge_count[0]
    live = alive.astype(jnp.float32)
    target = tail_owner[:, 0]
    target_hot = hot_rows(target, owners, jnp.float32)
    order = jnp.arange(edge_total, dtype=jnp.int32)
    before = (order[:, None] > order[None, :]).astype(jnp.bfloat16)
    earlier = jnp.dot(before, target_hot.astype(jnp.bfloat16), preferred_element_type=jnp.float32)
    slot_index = jnp.sum(earlier * target_hot, axis=1).astype(jnp.int32)
    position = target * capacity + slot_index
    slot_hot = hot_rows(position, owners * capacity, jnp.bfloat16)
    wanted = jnp.where(alive, tail_row, -1)
    taken = hot_rows(position, owners * capacity, jnp.int32)
    requests = jnp.sum(taken * (wanted + 1)[:, None], axis=0) - 1
    requested = deal(requests.reshape(owners, capacity), "blk").reshape(-1)

    table = entities.astype(jnp.bfloat16)
    own_block = pick(hot_rows(negative_rows[0], ent_count, jnp.bfloat16), table)
    located = pick(hot_rows(requested, ent_count, jnp.bfloat16), table)

    head_bf = pick(hot_rows(head_row, ent_count, jnp.bfloat16), table)
    rel_onehot = hot_rows(relation_id, rel_count, jnp.float32)
    rel_rows = jnp.dot(rel_onehot, relations, precision=lax.Precision.HIGHEST)
    head_f = head_bf.astype(jnp.float32)
    query_bf = complex_product(head_f, rel_rows).astype(jnp.bfloat16)
    query_f = query_bf.astype(jnp.float32)
    outgoing = lax.dot_general(
        slot_hot, query_bf, (((0,), (0,)), ((), ())), preferred_element_type=jnp.float32
    ).astype(jnp.bfloat16)
    returned, arrived, piece = forward_exchange(
        outgoing.reshape(owners, capacity, row_width),
        located.reshape(owners, capacity, row_width),
        own_block,
    )
    returned = returned.reshape(-1, row_width)
    piece = piece.reshape(-1, row_width)

    neg_scale = 1.0 / (owners * neg_count)
    scores = jnp.dot(query_bf, piece.T, preferred_element_type=jnp.float32)
    nweight = (neg_scale * live[:, None] * jax.nn.sigmoid(scores)).astype(jnp.bfloat16)
    neg_query = jnp.dot(nweight, piece, preferred_element_type=jnp.float32)
    neg_grads = jnp.dot(nweight.T, query_bf, preferred_element_type=jnp.float32)

    tail_bf = pick(slot_hot, arrived.reshape(owners * capacity, row_width))
    tail_f = tail_bf.astype(jnp.float32)
    weight = -live * jax.nn.sigmoid(-jnp.sum(query_f * tail_f, axis=1))
    grad_query = weight[:, None] * tail_f + neg_query
    grad_head, grad_rel = complex_grads(grad_query, head_f, rel_rows)
    rel_local = jnp.dot(rel_onehot.T, grad_rel, precision=lax.Precision.HIGHEST)
    late, rel_total = backward_exchange(
        neg_grads.reshape(owners, neg_count, row_width), rel_local, grad_head
    )
    new_relations = adagrad(relations, rel_total)

    returned_f = returned.astype(jnp.float32)
    owner_weight = -jax.nn.sigmoid(-jnp.sum(returned_f * located.astype(jnp.float32), axis=1))
    tail_rows = swap(requested)
    tail_weights = swap(owner_weight)
    tail_grads = tail_weights[:, None] * swap(returned).astype(jnp.float32)
    entity_grads = spread(tail_rows, ent_count, tail_grads)
    late_rows = jnp.concatenate([head_row, negative_rows[0]])
    late = late.reshape(-1, row_width)
    entity_grads = entity_grads + spread(swap(late_rows), ent_count, late)
    new_entities = adagrad(entities, entity_grads)
    return (new_entities, new_relations)


def solution(mesh):
    return jax.shard_map(
        per_device,
        mesh=mesh,
        in_specs=(
            P("blk", None),
            P(),
            P(("blk", "grp")),
            P(("blk", "grp")),
            P(("blk", "grp"), None),
            P(("blk", "grp")),
            P("blk", None),
            P(("blk", "grp")),
        ),
        out_specs=(P("blk", None), P()),
        check_vma=False,
    )
```

```python
import functools
import jax
import jax.numpy as jnp
from jax import lax
from jax.experimental import pallas as pl
from jax.experimental.pallas import tpu as pltpu
from jax.sharding import PartitionSpec as P

EPSILON = 1e-06
LEARN_RATE = 0.3


def complex_product(factor, other):
    half_width = factor.shape[1] // 2
    factor_real, factor_imag = (factor[:, :half_width], factor[:, half_width:])
    other_real, other_imag = (other[:, :half_width], other[:, half_width:])
    return jnp.concatenate(
        [
            factor_real * other_real - factor_imag * other_imag,
            factor_real * other_imag + factor_imag * other_real,
        ],
        axis=1,
    )


def complex_grads(upstream, head_vals, rel_vals):
    half_width = upstream.shape[1] // 2
    grad_real, grad_imag = (upstream[:, :half_width], upstream[:, half_width:])
    head_real, head_imag = (head_vals[:, :half_width], head_vals[:, half_width:])
    rel_real, rel_imag = (rel_vals[:, :half_width], rel_vals[:, half_width:])
    grad_head = jnp.concatenate(
        [grad_real * rel_real + grad_imag * rel_imag, grad_imag * rel_real - grad_real * rel_imag],
        axis=1,
    )
    grad_rel = jnp.concatenate(
        [
            grad_real * head_real + grad_imag * head_imag,
            grad_imag * head_real - grad_real * head_imag,
        ],
        axis=1,
    )
    return (grad_head, grad_rel)


def adagrad(table, table_grads):
    square_mean = jnp.mean(table_grads * table_grads, axis=1, keepdims=True)
    return table - LEARN_RATE * table_grads / (jnp.sqrt(square_mean) + EPSILON)


def hot_rows(index, count, dtype):
    return (index[:, None] == jnp.arange(count, dtype=jnp.int32)[None, :]).astype(dtype)


def pick(hot, table):
    return jnp.dot(hot, table, preferred_element_type=jnp.float32).astype(jnp.bfloat16)


def spread(rows, count, grads):
    hot = hot_rows(rows, count, jnp.bfloat16)
    high = lax.reduce_precision(grads, 8, 7)
    both = jnp.concatenate([high, grads - high], axis=1).astype(jnp.bfloat16)
    sums = lax.dot_general(
        hot, both, (((0,), (0,)), ((), ())), preferred_element_type=jnp.float32
    )
    width = grads.shape[1]
    return sums[:, :width] + sums[:, width:]


def swap(own):
    pairs = [(i, (i + 1) % lax.axis_size("grp")) for i in range(lax.axis_size("grp"))]
    other = lax.ppermute(own, "grp", pairs)
    first = lax.axis_index("grp") == 0
    return jnp.concatenate([jnp.where(first, own, other), jnp.where(first, other, own)], axis=0)


def deal(blocks, axes):
    return lax.all_to_all(blocks, axes, split_axis=0, concat_axis=0, tiled=True)


def remote(source, landing, send_sem, recv_sem, device):
    return pltpu.make_async_remote_copy(
        src_ref=source,
        dst_ref=landing,
        send_sem=send_sem,
        recv_sem=recv_sem,
        device_id=device,
        device_id_type=pl.DeviceIdType.MESH,
    )


def forward_kernel(
    owners, query_ref, tail_ref, own_ref, query_out, tail_out, neg_out, sends, recvs, passes, gots
):
    me = lax.axis_index("blk")
    sibling = me + 1 - 2 * lax.rem(me, 2)
    chips = owners // 2
    barrier = pltpu.get_barrier_semaphore()

    def hello(step, carry):
        pl.semaphore_signal(
            barrier,
            inc=1,
            device_id={"blk": lax.rem(me + step, owners)},
            device_id_type=pl.DeviceIdType.MESH,
        )
        return carry

    lax.fori_loop(1, owners, hello, 0)
    pl.semaphore_wait(barrier, owners - 1)

    def neg_copy(step):
        return remote(
            own_ref,
            neg_out.at[me],
            sends.at[0, step],
            recvs.at[0, step],
            {"blk": lax.rem(me + 2 * step, owners)},
        )

    def pass_copy(step):
        block = lax.rem(me - 2 * step + 2 * owners, owners)
        source = neg_out.at[block]
        return remote(source, source, passes.at[step], gots.at[step], {"blk": sibling})

    def row_copy(kind, source, landing, step):
        there = lax.rem(me + step, owners)
        return remote(
            source.at[there],
            landing.at[me],
            sends.at[kind, step],
            recvs.at[kind, step],
            {"blk": there},
        )

    def each(low, high, act):
        def body(step, carry):
            act(step)
            return carry

        lax.fori_loop(low, high, body, 0)

    neg_out[me] = own_ref[...]
    each(1, chips, lambda step: neg_copy(step).start())
    pass_copy(0).start()
    each(1, owners, lambda step: row_copy(1, tail_ref, tail_out, step).start())
    each(1, owners, lambda step: row_copy(2, query_ref, query_out, step).start())
    tail_out[me] = tail_ref[me]
    query_out[me] = query_ref[me]

    def hand_on(step):
        neg_copy(step).wait_recv()
        pass_copy(step).start()

    each(1, chips, hand_on)

    def finish(step):
        row_copy(1, tail_ref, tail_out, step).wait()
        row_copy(2, query_ref, query_out, step).wait()

    each(0, chips, lambda step: pass_copy(step).wait())
    each(1, chips, lambda step: neg_copy(step).wait_send())
    each(1, owners, finish)


def forward_exchange(outgoing, located, own_block):
    owners = outgoing.shape[0]
    vmem = pl.BlockSpec(memory_space=pltpu.VMEM)
    return pl.pallas_call(
        functools.partial(forward_kernel, owners),
        out_shape=(
            jax.ShapeDtypeStruct(outgoing.shape, jnp.bfloat16),
            jax.ShapeDtypeStruct(located.shape, jnp.bfloat16),
            jax.ShapeDtypeStruct((owners,) + own_block.shape, jnp.bfloat16),
        ),
        in_specs=[vmem] * 3,
        out_specs=(vmem,) * 3,
        scratch_shapes=[
            pltpu.SemaphoreType.DMA((3, owners)),
            pltpu.SemaphoreType.DMA((3, owners)),
            pltpu.SemaphoreType.DMA((owners,)),
            pltpu.SemaphoreType.DMA((owners,)),
        ],
        compiler_params=pltpu.CompilerParams(
            collective_id=1, has_side_effects=True, vmem_limit_bytes=48 * 2**20
        ),
    )(outgoing, located, own_block)


def backward_kernel(
    owners,
    bits,
    neg_ref,
    rel_ref,
    head_ref,
    late_out,
    rel_out,
    pre,
    staged,
    landed,
    rel_sums,
    rel_got,
    pre_send,
    pre_recv,
    part_send,
    part_recv,
    rel_send,
    rel_recv,
    grp_send,
    grp_recv,
):
    me = lax.axis_index("blk")
    group = lax.axis_index("grp")
    mate = {"grp": 1 - group}
    core = lax.rem(me, 2)
    chip = me // 2
    sibling = me + 1 - 2 * core
    chips = owners // 2
    head_count = head_ref.shape[0]
    neg_count = neg_ref.shape[1]
    barrier = pltpu.get_barrier_semaphore()

    def each(low, high, act):
        def body(step, carry):
            act(step)
            return carry

        lax.fori_loop(low, high, body, 0)

    def hello(step):
        pl.semaphore_signal(
            barrier,
            inc=1,
            device_id={"blk": lax.rem(me + step, owners)},
            device_id_type=pl.DeviceIdType.MESH,
        )

    each(1, owners, hello)
    pl.semaphore_signal(barrier, inc=1, device_id=mate, device_id_type=pl.DeviceIdType.MESH)
    pl.semaphore_wait(barrier, owners)

    def rel_copy(turn):
        if turn == bits:
            device = mate
        else:
            bit = 2**turn
            device = {"blk": me + bit - 2 * bit * lax.rem(me // bit, 2)}
        source = rel_ref if turn == 0 else rel_sums.at[turn - 1]
        return remote(source, rel_got.at[turn], rel_send.at[turn], rel_recv.at[turn], device)

    def rel_turn(turn):
        rel_copy(turn).wait_recv()
        source = rel_ref[...] if turn == 0 else rel_sums[turn - 1]
        if turn < bits:
            rel_sums[turn] = source + rel_got[turn]
            rel_copy(turn + 1).start()
        else:
            rel_out[...] = source + rel_got[turn]

    def pre_copy(step):
        there = lax.rem(chip + step, chips)
        return remote(
            neg_ref.at[2 * there + 1 - core],
            pre.at[there],
            pre_send.at[step],
            pre_recv.at[step],
            {"blk": sibling},
        )

    def part_copy(step):
        there = lax.rem(chip + step, chips)
        return remote(
            staged.at[there],
            landed.at[chip],
            part_send.at[step],
            part_recv.at[step],
            {"blk": 2 * there + core},
        )

    head_rows = late_out.at[group, pl.ds(0, head_count)]
    head_copy = remote(head_ref, head_rows, grp_send.at[0], grp_recv.at[0], mate)
    sum_rows = late_out.at[group, pl.ds(head_count, neg_count)]
    sum_copy = remote(sum_rows, sum_rows, grp_send.at[1], grp_recv.at[1], mate)

    rel_copy(0).start()
    each(0, chips, lambda step: pre_copy(step).start())
    head_copy.start()
    late_out[group, pl.ds(0, head_count)] = head_ref[...]
    rel_turn(0)

    def part(step):
        there = lax.rem(chip + step, chips)
        pre_copy(step).wait_recv()
        staged[there] = (neg_ref[2 * there + core] + pre[there]).astype(jnp.bfloat16)
        part_copy(step).start()

    each(1, chips, part)
    for turn in range(1, bits + 1):
        rel_turn(turn)
    pre_copy(0).wait_recv()
    late_out[group, pl.ds(head_count, neg_count)] = neg_ref[me] + pre[chip]

    def add(step):
        part_copy(step).wait_recv()
        origin = lax.rem(chip - step + chips, chips)
        late_out[group, pl.ds(head_count, neg_count)] += landed[origin].astype(jnp.float32)

    each(1, chips, add)
    sum_copy.start()
    for turn in range(bits + 1):
        rel_copy(turn).wait_send()
    each(0, chips, lambda step: pre_copy(step).wait_send())
    each(1, chips, lambda step: part_copy(step).wait_send())
    head_copy.wait()
    sum_copy.wait()


def backward_exchange(neg_parts, rel_local, grad_head):
    owners, neg_count, width = neg_parts.shape
    bits = owners.bit_length() - 1
    chips = owners // 2
    vmem = pl.BlockSpec(memory_space=pltpu.VMEM)
    late_count = grad_head.shape[0] + neg_count
    return pl.pallas_call(
        functools.partial(backward_kernel, owners, bits),
        out_shape=(
            jax.ShapeDtypeStruct((2, late_count, width), jnp.float32),
            jax.ShapeDtypeStruct(rel_local.shape, jnp.float32),
        ),
        in_specs=[vmem] * 3,
        out_specs=(vmem,) * 2,
        scratch_shapes=[
            pltpu.VMEM((chips, neg_count, width), jnp.float32),
            pltpu.VMEM((chips, neg_count, width), jnp.bfloat16),
            pltpu.VMEM((chips, neg_count, width), jnp.bfloat16),
            pltpu.VMEM((bits + 1,) + rel_local.shape, jnp.float32),
            pltpu.VMEM((bits + 1,) + rel_local.shape, jnp.float32),
            pltpu.SemaphoreType.DMA((chips,)),
            pltpu.SemaphoreType.DMA((chips,)),
            pltpu.SemaphoreType.DMA((chips,)),
            pltpu.SemaphoreType.DMA((chips,)),
            pltpu.SemaphoreType.DMA((bits + 1,)),
            pltpu.SemaphoreType.DMA((bits + 1,)),
            pltpu.SemaphoreType.DMA((2,)),
            pltpu.SemaphoreType.DMA((2,)),
        ],
        compiler_params=pltpu.CompilerParams(
            collective_id=2, has_side_effects=True, vmem_limit_bytes=48 * 2**20
        ),
    )(neg_parts, rel_local, grad_head)


def per_device(
    entities, relations, head_row, relation_id, tail_owner, tail_row, negative_rows, edge_count
):
    owners = lax.axis_size("blk")
    edge_total = head_row.shape[0]
    ent_count, row_width = entities.shape
    neg_count = negative_rows.shape[1]
    rel_count = relations.shape[0]
    capacity = -(-max(2, 2 * edge_total // owners) // 16) * 16
    alive = jnp.arange(edge_total, dtype=jnp.int32) < edge_count[0]
    live = alive.astype(jnp.float32)
    target = tail_owner[:, 0]
    target_hot = hot_rows(target, owners, jnp.float32)
    order = jnp.arange(edge_total, dtype=jnp.int32)
    before = (order[:, None] > order[None, :]).astype(jnp.bfloat16)
    earlier = jnp.dot(before, target_hot.astype(jnp.bfloat16), preferred_element_type=jnp.float32)
    slot_index = jnp.sum(earlier * target_hot, axis=1).astype(jnp.int32)
    position = target * capacity + slot_index
    slot_hot = hot_rows(position, owners * capacity, jnp.bfloat16)
    wanted = jnp.where(alive, tail_row, -1)
    taken = hot_rows(position, owners * capacity, jnp.int32)
    requests = jnp.sum(taken * (wanted + 1)[:, None], axis=0) - 1
    requested = deal(requests.reshape(owners, capacity), "blk").reshape(-1)

    table = entities.astype(jnp.bfloat16)
    own_block = pick(hot_rows(negative_rows[0], ent_count, jnp.bfloat16), table)
    located = pick(hot_rows(requested, ent_count, jnp.bfloat16), table)

    head_bf = pick(hot_rows(head_row, ent_count, jnp.bfloat16), table)
    rel_onehot = hot_rows(relation_id, rel_count, jnp.float32)
    rel_rows = jnp.dot(rel_onehot, relations, precision=lax.Precision.HIGHEST)
    head_f = head_bf.astype(jnp.float32)
    query_bf = complex_product(head_f, rel_rows).astype(jnp.bfloat16)
    query_f = query_bf.astype(jnp.float32)
    outgoing = lax.dot_general(
        slot_hot, query_bf, (((0,), (0,)), ((), ())), preferred_element_type=jnp.float32
    ).astype(jnp.bfloat16)
    returned, arrived, piece = forward_exchange(
        outgoing.reshape(owners, capacity, row_width),
        located.reshape(owners, capacity, row_width),
        own_block,
    )
    returned = returned.reshape(-1, row_width)
    piece = piece.reshape(-1, row_width)

    neg_scale = 1.0 / (owners * neg_count)
    scores = jnp.dot(query_bf, piece.T, preferred_element_type=jnp.float32)
    nweight = (neg_scale * live[:, None] * jax.nn.sigmoid(scores)).astype(jnp.bfloat16)
    neg_query = jnp.dot(nweight, piece, preferred_element_type=jnp.float32)
    neg_grads = jnp.dot(nweight.T, query_bf, preferred_element_type=jnp.float32)

    tail_bf = pick(slot_hot, arrived.reshape(owners * capacity, row_width))
    tail_f = tail_bf.astype(jnp.float32)
    weight = -live * jax.nn.sigmoid(-jnp.sum(query_f * tail_f, axis=1))
    grad_query = weight[:, None] * tail_f + neg_query
    grad_head, grad_rel = complex_grads(grad_query, head_f, rel_rows)
    rel_local = jnp.dot(rel_onehot.T, grad_rel, precision=lax.Precision.HIGHEST)
    late, rel_total = backward_exchange(
        neg_grads.reshape(owners, neg_count, row_width), rel_local, grad_head
    )
    new_relations = adagrad(relations, rel_total)

    returned_f = returned.astype(jnp.float32)
    owner_weight = -jax.nn.sigmoid(-jnp.sum(returned_f * located.astype(jnp.float32), axis=1))
    tail_rows = swap(requested)
    tail_weights = swap(owner_weight)
    tail_grads = tail_weights[:, None] * swap(returned).astype(jnp.float32)
    entity_grads = spread(tail_rows, ent_count, tail_grads)
    late_rows = jnp.concatenate([head_row, negative_rows[0]])
    late = late.reshape(-1, row_width)
    entity_grads = entity_grads + spread(swap(late_rows), ent_count, late)
    new_entities = adagrad(entities, entity_grads)
    return (new_entities, new_relations)


def solution(mesh):
    return jax.shard_map(
        per_device,
        mesh=mesh,
        in_specs=(
            P("blk", None),
            P(),
            P(("blk", "grp")),
            P(("blk", "grp")),
            P(("blk", "grp"), None),
            P(("blk", "grp")),
            P("blk", None),
            P(("blk", "grp")),
        ),
        out_specs=(P("blk", None), P()),
        check_vma=False,
    )
```
